512 devices in a mesh: dp: 8 (over z), cls: 64 (over y, x, core).
Axes of the slice: x: 4, y: 8, z: 8, core: 2. Of those that a mesh axis runs over, the one named last changes fastest.
Arguments:
- features: bfloat16 [4096, 6144], P(('dp', 'cls')), may hold values from -112 to 112
- basis: bfloat16 [2048, 6144], P('cls'), may hold values from -0.078125 to 0.078125
- weights: bfloat16 [2048, 16384], P(None, 'cls'), may hold values from -0.125 to 0.125
- labels: int32 [4096], P('dp'), may hold values from 0 to 16383
Outputs:
- losses: float32 [2, 4096], P(None, 'dp')
- grad_total: float32 [2048, 16384], P('dp', 'cls')
The draws below stay inside these ranges and needn't reach their ends.
All inputs are finite; a program needn't handle non-finite values.
Results may differ from the reference program's by a relative error of at most 0.014.
The reference program's roundings to bfloat16 on the way (of `whitened`, `residue` and `updated`) count: a program that leaves them out, or rounds other values in their place, can miss the bound.
Values may be sent and summed in bfloat16 or wider, within the bound.
No kernel may reach another device: no remote copies, remote signals or barrier semaphores. Data moves between devices by JAX's collectives and lax.ppermute only.
A program may use at most 64 MiB of HBM per device.

```python
import jax
import jax.numpy as jnp
from jax import lax

FEAT = 6144
WHITE = 2048
N_ROWS = 4096
CLASSES = 16384


def draw_features(key, part):
    key = jax.random.fold_in(key, 11)
    key_values, key_scales = jax.random.split(key)
    values = jnp.clip(jax.random.normal(key_values, (N_ROWS, FEAT), jnp.float32), -4.0, 4.0)
    scales = jnp.exp(jax.random.uniform(key_scales, (N_ROWS,), jnp.float32, jnp.log(0.5), jnp.log(2.0)))
    return (values * scales[:, None]).astype(jnp.bfloat16)


def touch_ends(result, own_key, smallest, high):
    shape = result.shape
    place = [jax.random.randint(jax.random.fold_in(own_key, axis), (), 0, shape[axis]) for axis in range(len(shape))]
    result = result.at[tuple(place)].set(smallest)
    longest = shape.index(max(shape))
    place[longest] = (place[longest] + 1) % shape[longest]
    return result.at[tuple(place)].set(high)


def levels(rng, dims, shards, low, high):
    def one(axis_at, parts):
        draws = jax.random.uniform(jax.random.fold_in(jax.random.fold_in(rng, 6), axis_at), (parts,), jnp.float32, low / len(shards), high / len(shards))
        return jnp.repeat(jnp.exp(draws), dims[axis_at] // parts).reshape((-1,) + (1,) * (len(dims) - axis_at - 1))

    loudness = one(*shards[0])
    for cut in shards[1:]:
        loudness = loudness * one(*cut)
    return loudness


def centred(stream_key, dims, spread, limit, cuts=(), kind=jnp.bfloat16):
    result = jax.random.normal(stream_key, dims, jnp.float32) * spread
    if len(cuts) > 0:
        result = levels(stream_key, dims, cuts, -0.22, 0.18) * result
    return jnp.clip(result, min=-limit, max=limit).astype(kind)


def setup_inputs(seed: int = 0) -> dict:
    splits = jax.random.split(jax.random.key(seed), 5)
    return {
        "features": draw_features(jax.random.fold_in(splits[4], 71), 0),
        "basis": centred(splits[1], (WHITE, FEAT), FEAT ** -0.5, 0.078125, ((0, 64),)),
        "weights": centred(splits[2], (WHITE, CLASSES), WHITE ** -0.5, 0.125, ((1, 64),)),
        "labels": touch_ends(jax.random.randint(splits[3], (N_ROWS,), 0, CLASSES), jax.random.fold_in(splits[3], 1), 0, CLASSES - 1).astype(jnp.int32),
    }


STEP_SCALE = 2.0


def one_pass(whitened, current, labels):
    logits = jnp.dot(whitened, current, preferred_element_type=jnp.float32)
    class_ids = jnp.arange(CLASSES, dtype=jnp.int32)
    target = labels[:, None] == class_ids[None, :]
    top = jnp.max(logits, axis=1)
    expo = jnp.exp(logits - top[:, None])
    total = jnp.sum(expo, axis=1)
    label_logit = jnp.sum(jnp.where(target, logits, 0.0), axis=1)
    losses = top + jnp.log(total) - label_logit
    residue = (expo / total[:, None] - target.astype(jnp.float32)).astype(jnp.bfloat16)
    gradient = lax.dot_general(whitened, residue, (((0,), (0,)), ((), ())), preferred_element_type=jnp.float32)
    return losses, gradient


def reference(features, basis, weights, labels):
    whitened = lax.dot_general(features, basis, (((1,), (1,)), ((), ())), preferred_element_type=jnp.float32).astype(jnp.bfloat16)
    losses_first, grad_first = one_pass(whitened, weights, labels)
    step_size = STEP_SCALE / WHITE
    updated = (weights.astype(jnp.float32) - step_size * grad_first).astype(jnp.bfloat16)
    losses_second, grad_second = one_pass(whitened, updated, labels)
    return jnp.stack([losses_first, losses_second]), grad_first + grad_second
```

```python
import jax
import jax.numpy as jnp
from jax import lax
from jax.sharding import Mesh
from jax.sharding import PartitionSpec as P

FEAT = 6144
WHITE = 2048
STEP_SCALE = 2.0
Z, Y, X, C = 8, 8, 4, 2
CLS = ("y", "x", "c")


def spread(block, axis, count):
    copies = jnp.broadcast_to(block[None], (count,) + block.shape)
    return lax.all_to_all(copies, axis, 0, 0, tiled=True)


def shards(features, basis, weights, labels):
    basis_rows = lax.all_gather(basis, "x", axis=0, tiled=True)
    image_rows = spread(spread(features, "y", Y), "c", C).reshape(C * Y * 8, FEAT)
    block = lax.dot_general(
        basis_rows, image_rows, (((1,), (1,)), ((), ())), preferred_element_type=jnp.float32
    ).astype(jnp.bfloat16)
    blocks = spread(spread(spread(block, "y", Y), "x", X), "c", C)
    blocks = blocks.reshape(C, X, Y, 4, 32, 128)
    white_t = blocks.transpose(2, 3, 0, 4, 1, 5).reshape(WHITE, 512)
    labels = labels.reshape(Y, X, C, 8).transpose(1, 2, 0, 3).reshape(512)

    width = weights.shape[1]
    class_ids = lax.axis_index(CLS) * width + lax.iota(jnp.int32, width)
    target = class_ids[:, None] == labels[None, :]
    step_size = STEP_SCALE / WHITE

    def forward(current):
        logits = lax.dot_general(
            current, white_t, (((0,), (0,)), ((), ())), preferred_element_type=jnp.float32
        )
        picked = jnp.sum(jnp.where(target, logits, 0.0), axis=0)
        own_top = jnp.max(logits, axis=0)
        own_lse = own_top + jnp.log(jnp.sum(jnp.exp(logits - own_top[None]), axis=0))
        parts = spread(jnp.stack([own_lse, picked]), CLS, Y * X * C)
        lses = parts[:, 0]
        top = jnp.max(lses, axis=0)
        lse = top + jnp.log(jnp.sum(jnp.exp(lses - top[None]), axis=0))
        losses = lse - jnp.sum(parts[:, 1], axis=0)
        residue = (jnp.exp(logits - lse[None]) - target.astype(jnp.float32)).astype(jnp.bfloat16)
        partial = lax.dot_general(
            white_t, residue, (((1,), (1,)), ((), ())), preferred_element_type=jnp.float32
        ).astype(jnp.bfloat16)
        pieces = lax.all_to_all(partial.reshape(Z, WHITE // Z, width), "z", 0, 0, tiled=True)
        return losses, jnp.sum(pieces.astype(jnp.float32), axis=0)

    losses_first, grad_first = forward(weights)
    own_rows = lax.dynamic_slice_in_dim(weights, lax.axis_index("z") * (WHITE // Z), WHITE // Z, 0)
    own_updated = (own_rows.astype(jnp.float32) - step_size * grad_first).astype(jnp.bfloat16)
    updated = spread(own_updated, "z", Z).reshape(WHITE, width)
    losses_second, grad_second = forward(updated)
    losses = jnp.stack([losses_first, losses_second])
    losses = losses.reshape(2, X, C, Y, 8).transpose(0, 3, 1, 2, 4).reshape(2, 512)
    return losses, grad_first + grad_second


def solution(mesh):
    fine = Mesh(mesh.devices.reshape(Z, Y, X, C), ("z", "y", "x", "c"))
    in_specs = (P(("z",) + CLS, None), P(CLS, None), P(None, CLS), P("z"))
    out_specs = (P(None, "z"), P("z", CLS))
    return jax.shard_map(shards, mesh=fine, in_specs=in_specs, out_specs=out_specs, check_vma=False)
```

```python
import jax
import jax.numpy as jnp
from jax import lax
from jax.sharding import Mesh
from jax.sharding import PartitionSpec as P

FEAT = 6144
WHITE = 2048
STEP_SCALE = 2.0
Z, Y, X, C = 8, 8, 4, 2
CLS = ("y", "x", "c")


def spread(block, axis, count):
    copies = jnp.broadcast_to(block[None], (count,) + block.shape)
    return lax.all_to_all(copies, axis, 0, 0, tiled=True)


def ring(block, axis, count):
    back = [[(at, (at - away) % count) for at in range(count)] for away in range(1, count)]
    return [block] + [lax.ppermute(block, axis, pairs) for pairs in back]


def in_order(rolled, axis, count):
    twice = jnp.concatenate([rolled, rolled])
    rows = rolled.shape[0]
    first = (count - lax.axis_index(axis)) * (rows // count)
    return lax.dynamic_slice_in_dim(twice, first, rows, 0)


def joined(parts):
    top = jnp.max(parts[:, 0], axis=0)
    total = jnp.sum(parts[:, 1] * jnp.exp(parts[:, 0] - top[None]), axis=0)
    return top, total, jnp.sum(parts[:, 2], axis=0)


def shards(features, basis, weights, labels):
    basis_rows = ring(basis, "x", X)
    image_rows = spread(spread(features, "y", Y), "c", C).reshape(C * Y * 8, FEAT)
    rolled = jnp.concatenate([
        lax.dot_general(rows, image_rows, (((1,), (1,)), ((), ())), preferred_element_type=jnp.float32)
        for rows in basis_rows
    ])
    block = in_order(rolled.astype(jnp.bfloat16), "x", X)
    blocks = spread(spread(spread(block, "y", Y), "x", X), "c", C)
    blocks = blocks.reshape(C, X, Y, 4, 32, 128)
    white_t = blocks.transpose(2, 3, 0, 4, 1, 5).reshape(WHITE, 512)
    labels = labels.reshape(Y, X, C, 8).transpose(1, 2, 0, 3).reshape(512)

    width = weights.shape[1]
    class_ids = lax.axis_index(CLS) * width + lax.iota(jnp.int32, width)
    target = class_ids[:, None] == labels[None, :]
    step_size = STEP_SCALE / WHITE

    def forward(current):
        logits = lax.dot_general(
            current, white_t, (((0,), (0,)), ((), ())), preferred_element_type=jnp.float32
        )
        picked = jnp.sum(jnp.where(target, logits, 0.0), axis=0)
        own_top = jnp.max(logits, axis=0)
        own_total = jnp.sum(jnp.exp(logits - own_top[None]), axis=0)
        own = jnp.stack([own_top, own_total, picked])
        other = lax.ppermute(own, "c", [(0, 1), (1, 0)])
        first = lax.axis_index("c") == 0
        pair = joined(jnp.stack([jnp.where(first, own, other), jnp.where(first, other, own)]))
        parts = spread(jnp.stack(pair).reshape(12, 128), ("y", "x"), Y * X)
        top, total, label_logit = joined(parts.reshape(Y * X, 3, 512))
        losses = top + jnp.log(total) - label_logit
        probs = jnp.exp(logits - top[None]) / total[None]
        residue = (probs - target.astype(jnp.float32)).astype(jnp.bfloat16)
        partial = lax.dot_general(
            white_t, residue, (((1,), (1,)), ((), ())), preferred_element_type=jnp.float32
        ).astype(jnp.bfloat16)
        pieces = lax.all_to_all(partial.reshape(Z, WHITE // Z, width), "z", 0, 0, tiled=True)
        return losses, jnp.sum(pieces.astype(jnp.float32), axis=0)

    losses_first, grad_first = forward(weights)
    own_rows = lax.dynamic_slice_in_dim(weights, lax.axis_index("z") * (WHITE // Z), WHITE // Z, 0)
    own_updated = (own_rows.astype(jnp.float32) - step_size * grad_first).astype(jnp.bfloat16)
    updated = spread(own_updated, "z", Z).reshape(WHITE, width)
    losses_second, grad_second = forward(updated)
    losses = jnp.stack([losses_first, losses_second])
    losses = losses.reshape(2, X, C, Y, 8).transpose(0, 3, 1, 2, 4).reshape(2, 512)
    return losses, grad_first + grad_second


def solution(mesh):
    fine = Mesh(mesh.devices.reshape(Z, Y, X, C), ("z", "y", "x", "c"))
    in_specs = (P(("z",) + CLS, None), P(CLS, None), P(None, CLS), P("z"))
    out_specs = (P(None, "z"), P("z", CLS))
    return jax.shard_map(shards, mesh=fine, in_specs=in_specs, out_specs=out_specs, check_vma=False)
```

```python
import jax
import jax.numpy as jnp
from jax import lax
from jax.sharding import Mesh
from jax.sharding import PartitionSpec as P

FEAT = 6144
WHITE = 2048
STEP_SCALE = 2.0
Z, Y, X, C = 8, 8, 4, 2
CLS = ("y", "x", "c")


def spread(block, axis, count):
    copies = jnp.broadcast_to(block[None], (count,) + block.shape)
    return lax.all_to_all(copies, axis, 0, 0, tiled=True)


def ring(block, axis, count):
    back = [[(at, (at - away) % count) for at in range(count)] for away in range(1, count)]
    return [block] + [lax.ppermute(block, axis, pairs) for pairs in back]


def in_order(rolled, axis, count):
    twice = jnp.concatenate([rolled, rolled])
    rows = rolled.shape[0]
    first = (count - lax.axis_index(axis)) * (rows // count)
    return lax.dynamic_slice_in_dim(twice, first, rows, 0)


def joined(parts):
    top = jnp.max(parts[:, 0], axis=0)
    total = jnp.sum(parts[:, 1] * jnp.exp(parts[:, 0] - top[None]), axis=0)
    return top, total, jnp.sum(parts[:, 2], axis=0)


def shards(features, basis, weights, labels):
    basis_rows = ring(basis, "x", X)
    own_images = spread(features, "y", Y).reshape(Y * 8, FEAT)
    other_images = lax.ppermute(own_images, "c", [(0, 1), (1, 0)])
    first = lax.axis_index("c") == 0
    own_part, other_part = [
        jnp.concatenate([
            lax.dot_general(rows, images, (((1,), (1,)), ((), ())), preferred_element_type=jnp.float32)
            for rows in basis_rows
        ])
        for images in (own_images, other_images)
    ]
    in_turn = jnp.where(first, own_part, other_part), jnp.where(first, other_part, own_part)
    block = in_order(jnp.concatenate(in_turn, axis=1).astype(jnp.bfloat16), "x", X)
    own = spread(spread(block, "y", Y), "x", X).reshape(X, Y, 4, 32, 128)
    other = lax.ppermute(own, "c", [(0, 1), (1, 0)])
    white_t = jnp.stack([jnp.where(first, own, other), jnp.where(first, other, own)], axis=3).reshape(X, WHITE, 128)
    labels = labels.reshape(Y, X, C, 8).transpose(1, 2, 0, 3).reshape(X, 128)

    width = weights.shape[1]
    class_ids = lax.axis_index(CLS) * width + lax.iota(jnp.int32, width)
    target = labels[:, :, None] == class_ids[None, None, :]
    step_size = STEP_SCALE / WHITE

    def forward(current):
        logits = lax.dot_general(
            white_t, current, (((1,), (0,)), ((), ())), preferred_element_type=jnp.float32
        )
        picked = jnp.sum(jnp.where(target, logits, 0.0), axis=2)
        own_top = jnp.max(logits, axis=2)
        own_total = jnp.sum(jnp.exp(logits - own_top[:, :, None]), axis=2)
        own = jnp.stack([own_top, own_total, picked])
        near = joined(spread(own, ("x", "c"), X * C))
        far = spread(jnp.stack(near), "y", Y)
        top, total, label_logit = joined(far)
        losses = top + jnp.log(total) - label_logit
        probs = jnp.exp(logits - top[:, :, None]) / total[:, :, None]
        residue = (probs - target.astype(jnp.float32)).astype(jnp.bfloat16)
        partial = lax.dot_general(
            white_t, residue, (((0, 2), (0, 1)), ((), ())), preferred_element_type=jnp.float32
        ).astype(jnp.bfloat16)
        pieces = lax.all_to_all(partial.reshape(Z, WHITE // Z, width), "z", 0, 0, tiled=True)
        return losses, jnp.sum(pieces.astype(jnp.float32), axis=0)

    losses_first, grad_first = forward(weights)
    own_rows = lax.dynamic_slice_in_dim(weights, lax.axis_index("z") * (WHITE // Z), WHITE // Z, 0)
    own_updated = (own_rows.astype(jnp.float32) - step_size * grad_first).astype(jnp.bfloat16)
    updated = spread(own_updated, "z", Z).reshape(WHITE, width)
    losses_second, grad_second = forward(updated)
    losses = jnp.stack([losses_first, losses_second])
    losses = losses.reshape(2, X, C, Y, 8).transpose(0, 3, 1, 2, 4).reshape(2, 512)
    return losses, grad_first + grad_second


def solution(mesh):
    fine = Mesh(mesh.devices.reshape(Z, Y, X, C), ("z", "y", "x", "c"))
    in_specs = (P(("z",) + CLS, None), P(CLS, None), P(None, CLS), P("z"))
    out_specs = (P(None, "z"), P("z", CLS))
    return jax.shard_map(shards, mesh=fine, in_specs=in_specs, out_specs=out_specs, check_vma=False)
```

```python
import jax
import jax.numpy as jnp
from jax import lax
from jax.sharding import Mesh
from jax.sharding import PartitionSpec as P

FEAT = 6144
WHITE = 2048
STEP_SCALE = 2.0
ZH, ZL, Y, X, C = 4, 2, 8, 4, 2
Z = ZH * ZL
DP = ("zh", "zl")
CLS = ("y", "x", "c")


def spread(block, axis, count):
    copies = jnp.broadcast_to(block[None], (count,) + block.shape)
    return lax.all_to_all(copies, axis, 0, 0, tiled=True)


def ring(block, axis, count):
    back = [[(at, (at - away) % count) for at in range(count)] for away in range(1, count)]
    return [block] + [lax.ppermute(block, axis, pairs) for pairs in back]


def in_order(rolled, axis, count):
    twice = jnp.concatenate([rolled, rolled])
    rows = rolled.shape[0]
    first = (count - lax.axis_index(axis)) * (rows // count)
    return lax.dynamic_slice_in_dim(twice, first, rows, 0)


def joined(parts):
    top = jnp.max(parts[:, 0], axis=0)
    total = jnp.sum(parts[:, 1] * jnp.exp(parts[:, 0] - top[None]), axis=0)
    return top, total, jnp.sum(parts[:, 2], axis=0)


def shards(features, basis, weights, labels):
    basis_rows = ring(basis, "x", X)
    own_images = spread(features, "y", Y).reshape(Y * 8, FEAT)
    other_images = lax.ppermute(own_images, "c", [(0, 1), (1, 0)])
    first = lax.axis_index("c") == 0
    own_part, other_part = [
        jnp.concatenate([
            lax.dot_general(rows, images, (((1,), (1,)), ((), ())), preferred_element_type=jnp.float32)
            for rows in basis_rows
        ])
        for images in (own_images, other_images)
    ]
    in_turn = jnp.where(first, own_part, other_part), jnp.where(first, other_part, own_part)
    block = in_order(jnp.concatenate(in_turn, axis=1).astype(jnp.bfloat16), "x", X)
    own = spread(spread(block, "y", Y), "x", X).reshape(X, Y, 4, 32, 128)
    other = lax.ppermute(own, "c", [(0, 1), (1, 0)])
    white_t = jnp.stack([jnp.where(first, own, other), jnp.where(first, other, own)], axis=3).reshape(X, WHITE, 128)
    parity = lax.axis_index("zl")
    white_near, white_far = [
        lax.dynamic_index_in_dim(white_t.reshape(X, ZH, ZL, WHITE // Z, 128), which, 2, keepdims=False).reshape(X, WHITE // 2, 128)
        for which in (parity, 1 - parity)
    ]
    labels = labels.reshape(Y, X, C, 8).transpose(1, 2, 0, 3).reshape(X, 128)

    width = weights.shape[1]
    class_ids = lax.axis_index(CLS) * width + lax.iota(jnp.int32, width)
    target = labels[:, :, None] == class_ids[None, None, :]
    step_size = STEP_SCALE / WHITE

    def product(white, current):
        return lax.dot_general(white, current, (((1,), (0,)), ((), ())), preferred_element_type=jnp.float32)

    def forward(logits):
        picked = jnp.sum(jnp.where(target, logits, 0.0), axis=2)
        own_top = jnp.max(logits, axis=2)
        own_total = jnp.sum(jnp.exp(logits - own_top[:, :, None]), axis=2)
        own = jnp.stack([own_top, own_total, picked])
        near = joined(spread(own, ("x", "c"), X * C))
        far = spread(jnp.stack(near), "y", Y)
        top, total, label_logit = joined(far)
        losses = top + jnp.log(total) - label_logit
        probs = jnp.exp(logits - top[:, :, None]) / total[:, :, None]
        residue = (probs - target.astype(jnp.float32)).astype(jnp.bfloat16)
        partial = lax.dot_general(
            white_t, residue, (((0, 2), (0, 1)), ((), ())), preferred_element_type=jnp.float32
        ).astype(jnp.bfloat16)
        pieces = lax.all_to_all(partial.reshape(Z, WHITE // Z, width), DP, 0, 0, tiled=True)
        return losses, jnp.sum(pieces.astype(jnp.float32), axis=0)

    losses_first, grad_first = forward(product(white_t, weights))
    own_rows = lax.dynamic_slice_in_dim(weights, lax.axis_index(DP) * (WHITE // Z), WHITE // Z, 0)
    own_updated = (own_rows.astype(jnp.float32) - step_size * grad_first).astype(jnp.bfloat16)
    half = width // 2
    near = spread(own_updated, "zh", ZH).reshape(WHITE // 2, width)
    ahead = lax.ppermute(near[:, :half], DP, [(at, (at - 1) % Z) for at in range(Z)])
    behind = lax.ppermute(near[:, half:], DP, [(at, (at + 1) % Z) for at in range(Z)])
    logits = product(white_near, near)
    logits = logits + jnp.concatenate([product(white_far, ahead), product(white_far, behind)], axis=2)
    losses_second, grad_second = forward(logits)
    losses = jnp.stack([losses_first, losses_second])
    losses = losses.reshape(2, X, C, Y, 8).transpose(0, 3, 1, 2, 4).reshape(2, 512)
    return losses, grad_first + grad_second


def solution(mesh):
    fine = Mesh(mesh.devices.reshape(ZH, ZL, Y, X, C), DP + CLS)
    in_specs = (P(DP + CLS, None), P(CLS, None), P(None, CLS), P(DP))
    out_specs = (P(None, DP), P(DP, CLS))
    return jax.shard_map(shards, mesh=fine, in_specs=in_specs, out_specs=out_specs, check_vma=False)
```
